128 devices in a mesh: tm: 4 (over z_lo, core), tile: 32 (over y, x, z_hi).
Axes of the slice: x: 4, y: 4, z: 4 (z_hi: 2, z_lo: 2; z = z_hi * 2 + z_lo), core: 2. Of those that a mesh axis runs over, the one named last changes fastest.
Arguments:
- pcs: float32 [2, 256], P(None, 'tm'), may hold values from -6 to 6
- st_eof: float32 [2, 120, 512], replicated, may hold values from -6 to 6
- spatial_eof: bfloat16 [2, 512, 256, 2048], P(None, 'tm', 'tile'), may hold values from -1 to 1
- land_sea: int32 [256, 2048], P('tile'), may hold values 0 or 1
Outputs:
- vorticity: float32 [256, 256, 2048], P('tm', 'tile')
- divergence: float32 [256, 256, 2048], P('tm', 'tile')
The draws below stay inside these ranges and needn't reach their ends.
All inputs are finite; a program needn't handle non-finite values. No bound on the sum of `land_sea` on one device may be relied on, other than what follows from the above.
Results may differ from the reference program's by a relative error of at most 0.0041.
Values may be sent and summed in bfloat16 or wider, within the bound.
No kernel may reach another device: no remote copies, remote signals or barrier semaphores. Data moves between devices by JAX's collectives and lax.ppermute only.
A program may use at most 128 MiB of HBM per device.

```python
import math
import jax
import jax.numpy as jnp
from jax import lax

C = 512
M = 120
K = 2
NLON = 2048
DAYS = 256
NLAT = 256


def with_ends(array, key, low, high):
    extent = array.shape
    place = [jax.random.randint(jax.random.fold_in(key, axis), (), 0, extent[axis]) for axis in range(len(extent))]
    array = array.at[tuple(place)].set(low)
    longest = extent.index(max(extent))
    place[longest] = (place[longest] + 1) % extent[longest]
    return array.at[tuple(place)].set(high)


def levels(rng, shape, pieces, least, high):
    loudness = 1.0
    for axis_at, shards_of in pieces:
        heights = jax.random.uniform(jax.random.fold_in(jax.random.fold_in(rng, 6), axis_at), (shards_of,), jnp.float32, least / len(pieces), high / len(pieces))
        loudness = loudness * jnp.repeat(jnp.exp(heights), shape[axis_at] // shards_of).reshape((-1,) + (1,) * (len(shape) - 1 - axis_at))
    return loudness


def gaussian(stream_key, dims, width, reach, pieces=(), held_as=jnp.bfloat16):
    entries = width * jax.random.normal(stream_key, dims, jnp.float32)
    if pieces:
        entries = entries * levels(stream_key, dims, pieces, -0.22, 0.18)
    return jnp.clip(entries, -reach, reach).astype(held_as)


def setup_inputs(seed: int = 0) -> dict:
    key_list = jax.random.split(jax.random.key(seed), 5)
    return {
        "pcs": gaussian(key_list[0], (K, DAYS), 1.0, 6.0, ((1, 4),), jnp.float32),
        "st_eof": gaussian(key_list[1], (K, M, C), 1.0, 6.0, (), jnp.float32),
        "spatial_eof": gaussian(key_list[2], (2, C, NLAT, NLON), (C // 16) ** -0.5, 1.0, ((1, 4), (2, 32))),
        "land_sea": with_ends((jax.random.randint(key_list[3], (NLAT, NLON), 0, 4) < 3).astype(jnp.int32), jax.random.fold_in(key_list[3], 1), 0, 1),
    }


def lagged_rc(series, st_eof, first, count):
    day_index = first + jnp.arange(count, dtype=jnp.int32)
    lag_steps = jnp.arange(M, dtype=jnp.int32)
    lag_index = day_index[:, None] - lag_steps[None, :]
    inside = lag_index >= 0
    safe_index = jnp.maximum(lag_index, 0)
    values_lag = jnp.where(inside[None], series[:, safe_index], 0.0)
    lagged = jnp.transpose(values_lag, (1, 0, 2)).reshape(count, K * M)
    lagged_sums = jnp.dot(lagged, st_eof.reshape(K * M, -1), precision=lax.Precision.HIGHEST, preferred_element_type=jnp.float32)
    window_len = jnp.minimum(day_index + 1, M).astype(lagged_sums.dtype)
    return lagged_sums / window_len[:, None]


def curl_div(east_pad, north_pad, latitude):
    cosine = jnp.cos(latitude)
    cos_east = east_pad * cosine[None, :, None]
    cos_north = north_pad * cosine[None, :, None]
    inner_east = east_pad[:, 1:-1]
    inner_north = north_pad[:, 1:-1]
    zonal_east = jnp.roll(inner_east, -1, axis=2) - jnp.roll(inner_east, 1, axis=2)
    zonal_north = jnp.roll(inner_north, -1, axis=2) - jnp.roll(inner_north, 1, axis=2)
    denominator = 2.0 * cosine[1:-1][None, :, None]
    vorticity = (zonal_north - (cos_east[:, 2:] - cos_east[:, :-2])) / denominator
    divergence = (zonal_east + (cos_north[:, 2:] - cos_north[:, :-2])) / denominator
    return vorticity, divergence


def reference(pcs, st_eof, spatial_eof, land_sea):
    components = lagged_rc(pcs, st_eof, 0, DAYS).astype(jnp.bfloat16)
    cell_count = NLAT * NLON
    ocean_mask = land_sea.astype(jnp.float32)
    east_vel = jnp.dot(components, spatial_eof[0].reshape(C, cell_count), preferred_element_type=jnp.float32).reshape(DAYS, NLAT, NLON)
    north_vel = jnp.dot(components, spatial_eof[1].reshape(C, cell_count), preferred_element_type=jnp.float32).reshape(DAYS, NLAT, NLON)
    east_vel = (east_vel * ocean_mask[None]).astype(jnp.bfloat16).astype(jnp.float32)
    north_vel = (north_vel * ocean_mask[None]).astype(jnp.bfloat16).astype(jnp.float32)
    east_pad = jnp.pad(east_vel, ((0, 0), (1, 1), (0, 0)))
    north_pad = jnp.pad(north_vel, ((0, 0), (1, 1), (0, 0)))
    global_rows = jnp.arange(-1, NLAT + 1, dtype=jnp.float32)
    latitude = (-70.0 + 140.0 * (global_rows + 0.5) / NLAT) * (math.pi / 180.0)
    vorticity, divergence = curl_div(east_pad, north_pad, latitude)
    return vorticity * ocean_mask[None], divergence * ocean_mask[None]
```

```python
import functools
import math

import jax
import jax.numpy as jnp
from jax import lax
from jax.experimental import pallas as pl
from jax.experimental.pallas import tpu as pltpu
from jax.sharding import PartitionSpec as P

F32 = jnp.float32
BF16 = jnp.bfloat16
VMEM = pltpu.VMEM
DAY_CHUNK = 16
LON_BLOCK = 512


def iota(shape, dim):
    return lax.broadcasted_iota(jnp.int32, shape, dim)


def components_kernel(place, pcs_ref, st_ref, comp_ref, all_ref):
    pairs, lags, _ = st_ref.shape
    days = pcs_ref.shape[1]
    share = comp_ref.shape[1] // 2
    window = jnp.minimum(iota((days, share), 0) + 1, lags).astype(F32)
    lagged = []
    for k in range(pairs):
        row = jnp.concatenate([jnp.zeros((1, 128), F32), pcs_ref[pl.ds(k, 1), :], jnp.zeros((1, 128), F32)], axis=1)
        wide = jnp.broadcast_to(row, (lags, days + 256))
        shifted = pltpu.roll(wide, 0, 1, stride=1, stride_axis=0)
        lagged.append(shifted[:, 128:128 + days].T)
    for half in range(2):
        first = pl.multiple_of(place[2 + half], share)
        total = jnp.zeros((days, share), F32)
        for k in range(pairs):
            total += jnp.dot(lagged[k], st_ref[k, :, pl.ds(first, share)], precision=lax.Precision.HIGHEST, preferred_element_type=F32)
        all_ref[...] = total / window
        count = comp_ref.shape[0] // 2
        for side in range(2):
            rows = all_ref[pl.ds(pl.multiple_of(place[side], count), count), :]
            comp_ref[side * count:(side + 1) * count, half * share:(half + 1) * share] = rows.astype(BF16)


def spread(comp, lat):
    share = comp.shape[1]
    shape = (share, share * lat)
    rep = jnp.where(iota(shape, 1) // lat == iota(shape, 0), 1.0, 0.0).astype(BF16)
    return jnp.dot(comp, rep, preferred_element_type=F32)


def only_row(wide, row, lat):
    return jnp.where(iota(wide.shape, 1) % lat == row, wide, 0.0).astype(BF16)


def edge_kernel(lat, comp_ref, own_ref, oth_ref, send_ref, keep_ref, x_ref):
    days, chans = comp_ref.shape
    share = chans // 2
    depth = share * lat

    @pl.when(pl.program_id(0) == 0)
    def _():
        for half in range(2):
            wide = spread(comp_ref[:, half * share:(half + 1) * share], lat)
            for side, row in enumerate((0, lat - 1)):
                x_ref[side * days:(side + 1) * days, half * depth:(half + 1) * depth] = only_row(wide, row, lat)

    acc = jnp.dot(x_ref[:, :depth], own_ref[0], preferred_element_type=F32)
    acc += jnp.dot(x_ref[:, depth:], oth_ref[0], preferred_element_type=F32)
    send_ref[...] = acc.astype(BF16)
    for side in range(2):
        keep_ref[side] = acc[side * days:side * days + days // 2]


def edge_call(comp, own, oth, x, lat, block):
    days = comp.shape[0]
    depth, lon = own.shape[1:]
    return pl.pallas_call(
        functools.partial(edge_kernel, lat),
        grid=(lon // block,),
        in_specs=[
            pl.BlockSpec(comp.shape, lambda n: (0, 0)),
            pl.BlockSpec((1, depth, block), lambda n: (x, 0, n)),
            pl.BlockSpec((1, depth, block), lambda n: (0, 0, n)),
        ],
        out_specs=[
            pl.BlockSpec((2 * days, block), lambda n: (0, n)),
            pl.BlockSpec((2, days // 2, block), lambda n: (0, 0, n)),
        ],
        out_shape=[
            jax.ShapeDtypeStruct((2 * days, lon), BF16),
            jax.ShapeDtypeStruct((2, days // 2, lon), F32),
        ],
        scratch_shapes=[VMEM((2 * days, 2 * depth), BF16)],
        compiler_params=pltpu.CompilerParams(vmem_limit_bytes=40 << 20),
        cost_estimate=pl.CostEstimate(flops=2 * 2 * days * 2 * depth * lon, bytes_accessed=4 * depth * lon + 8 * days * lon, transcendentals=0),
        name="edge_partials",
    )(comp, own, oth)


def inner_kernel(lat, first, chunk, comp_ref, own_ref, oth_u_ref, oth_v_ref, send_ref, keep_ref, x_ref):
    days, chans = comp_ref.shape
    share = chans // 2
    depth = share * lat
    inner = (lat - 2) * chunk

    @pl.when((pl.program_id(0) == 0) & (pl.program_id(1) == 0))
    def _():
        for half in range(2):
            chan = slice(half * share, (half + 1) * share)
            cols = slice(half * depth, (half + 1) * depth)
            wide = spread(comp_ref[first:first + chunk, chan], lat)
            for row in range(1, lat - 1):
                x_ref[(row - 1) * chunk:row * chunk, cols] = only_row(wide, row, lat)
            wide = spread(comp_ref[days // 2 + first:days // 2 + first + chunk, chan], lat)
            shape = (chunk, lat, depth)
            tall = jnp.where(iota(shape, 2) % lat == iota(shape, 1), jnp.broadcast_to(wide[:, None, :], shape), 0.0)
            x_ref[inner:, cols] = tall.reshape(chunk * lat, depth).astype(BF16)

    def add(oth_ref):
        acc = jnp.dot(x_ref[:, :depth], own_ref[0], preferred_element_type=F32)
        acc += jnp.dot(x_ref[:, depth:], oth_ref[0], preferred_element_type=F32)
        send_ref[0] = acc[:inner].astype(BF16)
        keep_ref[0] = acc[inner:]

    pl.when(pl.program_id(0) == 0)(lambda: add(oth_u_ref))
    pl.when(pl.program_id(0) == 1)(lambda: add(oth_v_ref))


def inner_call(comp, own, oth_u, oth_v, lat, first, chunk, block):
    depth, lon = own.shape[1:]
    steps = lon // block
    inner = (lat - 2) * chunk
    rows = inner + lat * chunk
    return pl.pallas_call(
        functools.partial(inner_kernel, lat, first, chunk),
        grid=(2, steps),
        in_specs=[
            pl.BlockSpec(comp.shape, lambda x, n: (0, 0)),
            pl.BlockSpec((1, depth, block), lambda x, n: (x, 0, n)),
            pl.BlockSpec((1, depth, block), lambda x, n: (0, 0, jnp.where(x == 0, n, steps - 1))),
            pl.BlockSpec((1, depth, block), lambda x, n: (0, 0, jnp.where(x == 1, n, 0))),
        ],
        out_specs=[
            pl.BlockSpec((1, inner, block), lambda x, n: (x, 0, n)),
            pl.BlockSpec((1, lat * chunk, block), lambda x, n: (x, 0, n)),
        ],
        out_shape=[
            jax.ShapeDtypeStruct((2, inner, lon), BF16),
            jax.ShapeDtypeStruct((2, lat * chunk, lon), F32),
        ],
        scratch_shapes=[VMEM((rows, 2 * depth), BF16)],
        compiler_params=pltpu.CompilerParams(vmem_limit_bytes=40 << 20),
        cost_estimate=pl.CostEstimate(flops=2 * rows * 2 * depth * 2 * lon, bytes_accessed=8 * depth * lon + 2 * lon * (2 * inner + 4 * lat * chunk), transcendentals=0),
        name="inner_partials",
    )(comp, own, oth_u, oth_v)


def select(shape, of_row, of_col):
    row, col = iota(shape, 0), iota(shape, 1)
    return jnp.where(of_row(row) == of_col(col), 1.0, 0.0).astype(BF16)


def curl_kernel(lat, chunk, keep_ref, inner_ref, edge_u_ref, edge_v_ref, low_u_ref, low_v_ref, high_u_ref, high_v_ref, land_ref, coef_ref, *rest):
    vort_ref, div_ref = rest[-2:]
    lon = land_ref.shape[1]
    rows = chunk * lat
    mask = land_ref[...].astype(F32)
    from_inner = select((rows, (lat - 2) * chunk), lambda r: (r % lat) * chunk + r // lat, lambda c: c + chunk)
    from_low = select((rows, chunk), lambda r: (r % lat) * chunk + r // lat, lambda c: c)
    from_high = select((rows, chunk), lambda r: (r % lat) * chunk + r // lat, lambda c: c + (lat - 1) * chunk)
    up = jnp.where(iota((rows, rows), 0) % lat < lat - 1, jnp.where(iota((rows, rows), 1) == iota((rows, rows), 0) + 1, 1.0, 0.0), 0.0).astype(BF16)
    down = jnp.where(iota((rows, rows), 0) % lat > 0, jnp.where(iota((rows, rows), 1) + 1 == iota((rows, rows), 0), 1.0, 0.0), 0.0).astype(BF16)
    dot = functools.partial(jnp.dot, preferred_element_type=F32)
    zonal, merid = [], []
    cos_up = coef_ref[0][None, :, :1]
    cos_down = coef_ref[1][None, :, :1]
    scale = coef_ref[2][None, :, :1] * mask[None]
    for x in range(2):
        edge_ref = (edge_u_ref, edge_v_ref)[x]
        total = keep_ref[x] + dot(from_inner, inner_ref[x]) + dot(from_low, edge_ref[0]) + dot(from_high, edge_ref[1])
        vel = (total.reshape(chunk, lat, lon) * mask[None]).reshape(rows, lon).astype(BF16)
        above = dot(up, vel) + dot(from_high, (high_u_ref, high_v_ref)[x][...])
        below = dot(down, vel) + dot(from_low, (low_u_ref, low_v_ref)[x][...])
        wide = vel.astype(F32)
        zonal.append((pltpu.roll(wide, lon - 1, 1) - pltpu.roll(wide, 1, 1)).reshape(chunk, lat, lon))
        merid.append(cos_up * above.reshape(chunk, lat, lon) - cos_down * below.reshape(chunk, lat, lon))
    vort_ref[...] = (zonal[1] - merid[0]) * scale
    div_ref[...] = (zonal[0] + merid[1]) * scale


def curl_call(keep, inner, edges, halos, land, coef, outs, lat, days, at, chunk):
    lon = land.shape[1]
    day_rows = pl.BlockSpec((chunk, lon), lambda i: (at, 0))
    whole = lambda shape: pl.BlockSpec(shape, lambda i: (0,) * len(shape))
    out_spec = pl.BlockSpec((chunk, lat, lon), lambda i: (at, 0, 0))
    return pl.pallas_call(
        functools.partial(curl_kernel, lat, chunk),
        grid=(1,),
        in_specs=[whole(keep.shape), whole(inner.shape)]
        + [pl.BlockSpec((2, chunk, lon), lambda i: (0, at, 0))] * 2
        + [day_rows] * 4
        + [whole(land.shape), whole(coef.shape)]
        + [pl.BlockSpec(memory_space=pl.ANY)] * len(outs),
        out_specs=[out_spec] * 2,
        out_shape=[jax.ShapeDtypeStruct((days, lat, lon), F32)] * 2,
        input_output_aliases={10: 0, 11: 1} if outs else {},
        compiler_params=pltpu.CompilerParams(vmem_limit_bytes=56 << 20),
        cost_estimate=pl.CostEstimate(flops=20 * 2 * chunk * lat * lon, bytes_accessed=20 * chunk * lat * lon, transcendentals=0),
        name="curl_div",
    )(keep, inner, *edges, *halos, land, coef, *outs)


def shards(pcs, st_eof, spatial_eof, land_sea):
    day_dev = pcs.shape[1]
    _, share, lat, lon = spatial_eof.shape
    depth = share * lat
    tm = lax.axis_index("tm")
    tiles = lax.axis_size("tile")
    tile = lax.axis_index("tile")
    swap_core = [(i, i ^ 1) for i in range(4)]
    swap_chip = [(i, i ^ 2) for i in range(4)]
    north = [(t * tiles + i, (t ^ 2) * tiles + i + 1) for t in range(4) for i in range(tiles - 1)]
    south = [(t * tiles + i + 1, (t ^ 2) * tiles + i) for t in range(4) for i in range(tiles - 1)]

    own = spatial_eof.reshape(2, depth, lon)
    oth_u = lax.ppermute(own[0:1], "tm", swap_core)
    oth_v = lax.ppermute(own[1:2], "tm", swap_core)

    all_pcs = lax.all_gather(pcs, "tm", axis=1, tiled=True)
    place = jnp.stack([(tm ^ 2) * day_dev, tm * day_dev, tm * share, (tm ^ 1) * share]).astype(jnp.int32)
    comp = pl.pallas_call(
        components_kernel,
        in_specs=[pl.BlockSpec(memory_space=pltpu.SMEM)] + [pl.BlockSpec(memory_space=VMEM)] * 2,
        out_specs=pl.BlockSpec(memory_space=VMEM),
        out_shape=jax.ShapeDtypeStruct((2 * day_dev, 2 * share), BF16),
        scratch_shapes=[VMEM((all_pcs.shape[1], share), F32)],
        compiler_params=pltpu.CompilerParams(vmem_limit_bytes=24 << 20),
        name="components",
    )(place, all_pcs, st_eof)

    edges, keeps = [], []
    for x, oth in enumerate((oth_u, oth_v)):
        send, keep = edge_call(comp, own, oth, x, lat, LON_BLOCK)
        edges.append(lax.ppermute(send, "tm", swap_chip).reshape(2, 2 * day_dev, lon))
        keeps.append(keep)

    inners = []
    for first in range(0, day_dev, DAY_CHUNK):
        send, keep = inner_call(comp, own, oth_u, oth_v, lat, first, DAY_CHUNK, LON_BLOCK)
        inners.append((lax.ppermute(send, "tm", swap_chip), keep))

    ends = jnp.stack([land_sea[0], land_sea[lat - 1]]).astype(F32)[:, None, :]
    lows, highs = [], []
    for x in range(2):
        sums = keeps[x] + edges[x][:, day_dev:].astype(F32)
        vel = (sums * ends).astype(BF16)
        lows.append(lax.ppermute(vel[1], ("tm", "tile"), north))
        highs.append(lax.ppermute(vel[0], ("tm", "tile"), south))

    rows = (tile * lat).astype(F32) + jnp.arange(-1, lat + 1, dtype=F32)
    latitude = (-70.0 + 140.0 * (rows + 0.5) / (lat * tiles)) * (math.pi / 180.0)
    cosine = jnp.cos(latitude)
    coef = jnp.stack([cosine[2:], cosine[:-2], 0.5 / cosine[1:-1]])
    coef = jnp.broadcast_to(coef[:, :, None], (3, lat, 128))

    outs = []
    for at, (inner, keep) in enumerate(inners):
        outs = curl_call(keep, inner, edges, lows + highs, land_sea, coef, outs, lat, day_dev, at, DAY_CHUNK)
    return tuple(outs)


def solution(mesh):
    return jax.shard_map(
        shards,
        mesh=mesh,
        in_specs=(P(None, "tm"), P(), P(None, "tm", "tile", None), P("tile", None)),
        out_specs=(P("tm", "tile", None), P("tm", "tile", None)),
        check_vma=False,
    )
```

```python
import functools
import math

import jax
import jax.numpy as jnp
from jax import lax
from jax.experimental import pallas as pl
from jax.experimental.pallas import tpu as pltpu
from jax.sharding import PartitionSpec as P

F32 = jnp.float32
BF16 = jnp.bfloat16
VMEM = pltpu.VMEM
DAY_GROUPS = (32, 24, 8)
SUB_DAYS = 8
LON_BLOCK = 512
PIECES = (1, 3)
BLOCK_DAYS = 16
VMEM_LIMIT = 40 << 20


def iota(shape, dim):
    return lax.broadcasted_iota(jnp.int32, shape, dim)


def after(value, *earlier):
    return lax.optimization_barrier((value, *earlier))[0]


def spread(comp, lat):
    share = comp.shape[1]
    shape = (share, share * lat)
    rep = jnp.where(iota(shape, 1) // lat == iota(shape, 0), 1.0, 0.0).astype(BF16)
    return jnp.dot(comp, rep, preferred_element_type=F32)


def only_row(wide, row, lat):
    return jnp.where(iota(wide.shape, 1) % lat == row, wide, 0.0).astype(BF16)


def components_kernel(lat, place, *refs):
    pcs_refs, (st_ref, comp_ref, edge_ref, all_ref) = refs[:-4], refs[-4:]
    pairs, lags, _ = st_ref.shape
    day_dev = pcs_refs[0].shape[1]
    days = day_dev * len(pcs_refs)
    share = comp_ref.shape[1] // 2
    count = comp_ref.shape[0] // 2
    depth = share * lat
    lane_owner = iota((pairs, days), 1) // day_dev
    series = jnp.zeros((pairs, days), F32)
    for other, ref in enumerate(pcs_refs):
        tiled = jnp.concatenate([ref[...]] * len(pcs_refs), axis=1)
        series = jnp.where(lane_owner == place[4] ^ other, tiled, series)
    window = jnp.minimum(iota((days, share), 0) + 1, lags).astype(F32)
    lagged = []
    for k in range(pairs):
        row = jnp.concatenate([jnp.zeros((1, 128), F32), series[k:k + 1], jnp.zeros((1, 128), F32)], axis=1)
        wide = jnp.broadcast_to(row, (lags, days + 256))
        shifted = pltpu.roll(wide, 0, 1, stride=1, stride_axis=0)
        lagged.append(shifted[:, 128:128 + days].T)
    for half in range(2):
        first = pl.multiple_of(place[2 + half], share)
        total = jnp.zeros((days, share), F32)
        for k in range(pairs):
            total += jnp.dot(lagged[k], st_ref[k, :, pl.ds(first, share)], precision=lax.Precision.HIGHEST, preferred_element_type=F32)
        all_ref[...] = total / window
        for side in range(2):
            rows = all_ref[pl.ds(pl.multiple_of(place[side], count), count), :].astype(BF16)
            comp_ref[side * count:(side + 1) * count, half * share:(half + 1) * share] = rows
            wide = spread(rows, lat)
            for end, row in enumerate((0, lat - 1)):
                at = (2 * end + side) * count
                edge_ref[at:at + count, half * depth:(half + 1) * depth] = only_row(wide, row, lat)


def components_call(place, pcs_all, st_eof, share, lat):
    day_dev = pcs_all[0].shape[1]
    return pl.pallas_call(
        functools.partial(components_kernel, lat),
        in_specs=[pl.BlockSpec(memory_space=pltpu.SMEM)] + [pl.BlockSpec(memory_space=VMEM)] * (len(pcs_all) + 1),
        out_specs=[pl.BlockSpec(memory_space=VMEM)] * 2,
        out_shape=[
            jax.ShapeDtypeStruct((2 * day_dev, 2 * share), BF16),
            jax.ShapeDtypeStruct((4 * day_dev, 2 * share * lat), BF16),
        ],
        scratch_shapes=[VMEM((len(pcs_all) * day_dev, share), F32)],
        compiler_params=pltpu.CompilerParams(vmem_limit_bytes=12 << 20),
        name="components",
    )(place, *pcs_all, st_eof)


def edge_kernel(x_ref, own_ref, oth_ref, send_ref, keep_ref):
    rows = x_ref.shape[0]
    depth = own_ref.shape[1]
    acc = jnp.dot(x_ref[:, :depth], own_ref[0], preferred_element_type=F32)
    acc += jnp.dot(x_ref[:, depth:], oth_ref[0], preferred_element_type=F32)
    send_ref[0] = acc.astype(BF16)
    for end in range(2):
        keep_ref[0, end] = acc[end * rows // 2:end * rows // 2 + rows // 4]


def edge_call(x_edge, own, oth, first, width, block):
    rows = x_edge.shape[0]
    depth = oth.shape[1]
    at = first // block
    return pl.pallas_call(
        edge_kernel,
        grid=(width // block, 2),
        in_specs=[
            pl.BlockSpec(x_edge.shape, lambda n, x: (0, 0)),
            pl.BlockSpec((1, depth, block), lambda n, x: (x, 0, at + n)),
            pl.BlockSpec((1, depth, block), lambda n, x: (x, 0, at + n)),
        ],
        out_specs=[
            pl.BlockSpec((1, rows, block), lambda n, x: (x, 0, n)),
            pl.BlockSpec((1, 2, rows // 4, block), lambda n, x: (x, 0, 0, n)),
        ],
        out_shape=[
            jax.ShapeDtypeStruct((2, rows, width), BF16),
            jax.ShapeDtypeStruct((2, 2, rows // 4, width), F32),
        ],
        compiler_params=pltpu.CompilerParams(vmem_limit_bytes=57 << 20),
        cost_estimate=pl.CostEstimate(flops=2 * rows * 2 * depth * 2 * width, bytes_accessed=8 * depth * width + 8 * rows * width, transcendentals=0),
        name="edge_partials",
    )(x_edge, own, oth)


def inner_kernel(lat, first, span, pieces, comp_ref, own_ref, *refs):
    oth_refs, (send_ref, keep_ref, x_ref) = refs[:len(pieces)], refs[len(pieces):]
    days, chans = comp_ref.shape
    share = chans // 2
    depth = share * lat
    cut = send_ref.shape[1]

    @pl.when((pl.program_id(0) == 0) & (pl.program_id(1) == 0))
    def _():
        for half in range(2):
            chan = slice(half * share, (half + 1) * share)
            cols = slice(half * depth, (half + 1) * depth)
            wide = spread(comp_ref[first:first + span, chan], lat)
            tall = []
            for day in range(0, span, SUB_DAYS):
                tall += [only_row(wide[day:day + SUB_DAYS], row, lat) for row in range(1, lat - 1)]
            for at in range(0, len(tall), 2):
                x_ref[at * SUB_DAYS:(at + 2) * SUB_DAYS, cols] = jnp.concatenate(tall[at:at + 2], axis=0)
            wide = spread(comp_ref[days // 2 + first:days // 2 + first + span, chan], lat)
            shape = (span, lat, depth)
            tall = jnp.where(iota(shape, 2) % lat == iota(shape, 1), jnp.broadcast_to(wide[:, None, :], shape), 0.0)
            x_ref[cut:, cols] = tall.reshape(span * lat, depth).astype(BF16)

    def add(oth_ref):
        acc = jnp.dot(x_ref[:, :depth], own_ref[0], preferred_element_type=F32)
        acc += jnp.dot(x_ref[:, depth:], oth_ref[0], preferred_element_type=F32)
        send_ref[0] = acc[:cut].astype(BF16)
        keep_ref[0] = acc[cut:]

    start = 0
    for ref, piece in zip(oth_refs, pieces):
        inside = (pl.program_id(0) >= start) & (pl.program_id(0) < start + piece)
        pl.when(inside)(functools.partial(add, ref))
        start += piece


def inner_call(comp, own, oths, lat, first, span, block):
    depth, lon = own.shape[1:]
    pieces = [oth.shape[2] // block for oth in oths]
    rows = span * (2 * lat - 2)

    def piece_spec(start, piece):
        def at(n, x):
            before, past = n < start, n >= start + piece
            block_at = jnp.clip(n - start, 0, piece - 1)
            return (jnp.where(before, 0, jnp.where(past, 1, x)), 0, block_at)
        return pl.BlockSpec((1, depth, block), at)

    kinds = (((lat - 2) * span, BF16), (lat * span, F32))
    return pl.pallas_call(
        functools.partial(inner_kernel, lat, first, span, pieces),
        grid=(lon // block, 2),
        in_specs=[
            pl.BlockSpec(comp.shape, lambda n, x: (0, 0)),
            pl.BlockSpec((1, depth, block), lambda n, x: (x, 0, n)),
        ] + [piece_spec(sum(pieces[:i]), piece) for i, piece in enumerate(pieces)],
        out_specs=[pl.BlockSpec((1, height, block), lambda n, x: (x, 0, n)) for height, _ in kinds],
        out_shape=[jax.ShapeDtypeStruct((2, height, lon), dtype) for height, dtype in kinds],
        scratch_shapes=[VMEM((rows, 2 * depth), BF16)],
        compiler_params=pltpu.CompilerParams(vmem_limit_bytes=VMEM_LIMIT),
        cost_estimate=pl.CostEstimate(flops=2 * rows * 2 * depth * 2 * lon, bytes_accessed=8 * depth * lon + 6 * lon * rows, transcendentals=0),
        name="inner_partials",
    )(comp, own, *oths)


def halo_kernel(count, land_ref, *refs):
    keeps, edges, (low_ref, high_ref) = refs[:count], refs[count:2 * count], refs[2 * count:]
    lat, lon = land_ref.shape
    days = low_ref.shape[1]
    start = 0
    for keep, edge in zip(keeps, edges):
        width = keep.shape[3]
        for end, out in ((lat - 1, low_ref), (0, high_ref)):
            side = int(end > 0)
            mask = land_ref[end:end + 1, start:start + width].astype(F32)
            for x in range(2):
                total = keep[x, side] + edge[x, (2 * side + 1) * days:(2 * side + 2) * days, :].astype(F32)
                out[x, :, start:start + width] = (total * mask).astype(BF16)
        start += width


def halo_call(land, keeps, edges):
    days = keeps[0].shape[2]
    shape = jax.ShapeDtypeStruct((2, days, land.shape[1]), BF16)
    return pl.pallas_call(
        functools.partial(halo_kernel, len(keeps)),
        in_specs=[pl.BlockSpec(memory_space=VMEM)] * (1 + 2 * len(keeps)),
        out_specs=[pl.BlockSpec(memory_space=VMEM)] * 2,
        out_shape=[shape] * 2,
        compiler_params=pltpu.CompilerParams(vmem_limit_bytes=VMEM_LIMIT),
        cost_estimate=pl.CostEstimate(flops=8 * days * land.shape[1], bytes_accessed=48 * days * land.shape[1], transcendentals=0),
        name="halo_rows",
    )(land, *keeps, *edges)


def select(shape, of_row, of_col):
    row, col = iota(shape, 0), iota(shape, 1)
    return jnp.where(of_row(row) == of_col(col), 1.0, 0.0).astype(BF16)


def curl_kernel(lat, first, count, keep_ref, inner_ref, low_ref, high_ref, land_ref, coef_ref, *rest):
    edges, (vort_ref, div_ref) = rest[:count], rest[-2:]
    lon = land_ref.shape[1]
    chunk = SUB_DAYS
    rows = chunk * lat
    seen = low_ref.shape[1]
    skip = (first + pl.program_id(0) * chunk) % seen
    mask = land_ref[...].astype(F32)
    from_inner = select((rows, (lat - 2) * chunk), lambda r: (r % lat) * chunk + r // lat, lambda c: c + chunk)
    from_low = select((rows, seen), lambda r: (r % lat) * seen + r // lat + skip, lambda c: c)
    from_high = select((rows, seen), lambda r: (r % lat) * seen + r // lat + skip, lambda c: c + (lat - 1) * seen)
    row, col = iota((rows, rows), 0), iota((rows, rows), 1)
    up = jnp.where(row % lat < lat - 1, jnp.where(col == row + 1, 1.0, 0.0), 0.0).astype(BF16)
    down = jnp.where(row % lat > 0, jnp.where(col + 1 == row, 1.0, 0.0), 0.0).astype(BF16)
    dot = functools.partial(jnp.dot, preferred_element_type=F32)
    zonal, merid = [], []
    cos_up = coef_ref[0][None, :, :1]
    cos_down = coef_ref[1][None, :, :1]
    scale = coef_ref[2][None, :, :1] * mask[None]
    for x in range(2):
        ends = [dot(from_low, e[x, 0]) + dot(from_high, e[x, 1]) for e in edges]
        total = keep_ref[x] + dot(from_inner, inner_ref[x]) + jnp.concatenate(ends, axis=1)
        vel = (total.reshape(chunk, lat, lon) * mask[None]).reshape(rows, lon).astype(BF16)
        above = dot(up, vel) + dot(from_high, high_ref[x])
        below = dot(down, vel) + dot(from_low, low_ref[x])
        wide = vel.astype(F32)
        zonal.append((pltpu.roll(wide, lon - 1, 1) - pltpu.roll(wide, 1, 1)).reshape(chunk, lat, lon))
        merid.append(cos_up * above.reshape(chunk, lat, lon) - cos_down * below.reshape(chunk, lat, lon))
    vort_ref[...] = (zonal[1] - merid[0]) * scale
    div_ref[...] = (zonal[0] + merid[1]) * scale


def curl_call(keep, inner, edges, halos, land, coef, outs, lat, days, first, span):
    lon = land.shape[1]
    per = BLOCK_DAYS // SUB_DAYS
    block = first // SUB_DAYS
    whole = lambda shape: pl.BlockSpec(shape, lambda i: (0,) * len(shape))
    out_spec = pl.BlockSpec((SUB_DAYS, lat, lon), lambda i: (block + i, 0, 0))
    return pl.pallas_call(
        functools.partial(curl_kernel, lat, first, len(edges)),
        grid=(span // SUB_DAYS,),
        in_specs=[
            pl.BlockSpec((2, lat * SUB_DAYS, lon), lambda i: (0, i, 0)),
            pl.BlockSpec((2, (lat - 2) * SUB_DAYS, lon), lambda i: (0, i, 0)),
        ]
        + [pl.BlockSpec((2, BLOCK_DAYS, lon), lambda i: (0, (block + i) // per, 0))] * 2
        + [whole(land.shape), whole(coef.shape)]
        + [pl.BlockSpec((2, 2, BLOCK_DAYS, e.shape[3]), lambda i: (0, 0, (block + i) // per, 0)) for e in edges]
        + [pl.BlockSpec(memory_space=pl.ANY)] * len(outs),
        out_specs=[out_spec] * 2,
        out_shape=[jax.ShapeDtypeStruct((days, lat, lon), F32)] * 2,
        input_output_aliases={6 + len(edges): 0, 7 + len(edges): 1} if outs else {},
        compiler_params=pltpu.CompilerParams(vmem_limit_bytes=VMEM_LIMIT),
        cost_estimate=pl.CostEstimate(flops=20 * 2 * span * lat * lon, bytes_accessed=20 * span * lat * lon, transcendentals=0),
        name="curl_div",
    )(keep, inner, *halos, land, coef, *edges, *outs)


def shards(pcs, st_eof, spatial_eof, land_sea):
    day_dev = pcs.shape[1]
    _, share, lat, lon = spatial_eof.shape
    depth = share * lat
    tm = lax.axis_index("tm")
    tiles = lax.axis_size("tile")
    tile = lax.axis_index("tile")
    swap_core = [(i, i ^ 1) for i in range(4)]
    swap_chip = [(i, i ^ 2) for i in range(4)]
    north = [(t * tiles + i, (t ^ 2) * tiles + i + 1) for t in range(4) for i in range(tiles - 1)]
    south = [(t * tiles + i + 1, (t ^ 2) * tiles + i) for t in range(4) for i in range(tiles - 1)]

    pcs_all = [pcs] + [lax.ppermute(pcs, "tm", [(i, i ^ s) for i in range(4)]) for s in (1, 2, 3)]
    own = spatial_eof.reshape(2, depth, lon)
    widths = [LON_BLOCK * piece for piece in PIECES]
    spans = [(sum(widths[:i]), width) for i, width in enumerate(widths)]
    oth = lax.ppermute(after(own, pcs_all[1]), "tm", swap_core)

    place = jnp.stack([(tm ^ 2) * day_dev, tm * day_dev, tm * share, (tm ^ 1) * share, tm]).astype(jnp.int32)
    comp, x_edge = components_call(place, pcs_all, st_eof, share, lat)

    edges, keeps = [], []
    for start, width in spans:
        send, keep = edge_call(x_edge, own, oth, start, width, LON_BLOCK)
        x_edge = after(x_edge, send)
        edges.append(lax.ppermute(send, "tm", swap_chip))
        keeps.append(keep)

    inners = []
    first = 0
    sent = list(edges)
    for span in DAY_GROUPS:
        comp = after(comp, send, sent[-2])
        if len(sent) == len(edges) + 1:
            low, high = halo_call(after(land_sea, send), keeps, edges)
            comp = after(comp, low)
            halos = [lax.ppermute(low, ("tm", "tile"), north), lax.ppermute(high, ("tm", "tile"), south)]
        send, keep = inner_call(comp, own, [oth], lat, first, span, LON_BLOCK)
        sent.append(lax.ppermute(send, "tm", swap_chip))
        inners.append((sent[-1], keep))
        first += span

    rows = (tile * lat).astype(F32) + jnp.arange(-1, lat + 1, dtype=F32)
    latitude = (-70.0 + 140.0 * (rows + 0.5) / (lat * tiles)) * (math.pi / 180.0)
    cosine = jnp.cos(latitude)
    coef = jnp.stack([cosine[2:], cosine[:-2], 0.5 / cosine[1:-1]])
    coef = jnp.broadcast_to(coef[:, :, None], (3, lat, 128))

    edges = [e.reshape(2, 2, 2 * day_dev, -1) for e in edges]
    outs = []
    first = 0
    for span, (inner, keep) in zip(DAY_GROUPS, inners):
        outs = curl_call(keep, inner, edges, halos, land_sea, coef, outs, lat, day_dev, first, span)
        first += span
    return tuple(outs)


def solution(mesh):
    return jax.shard_map(
        shards,
        mesh=mesh,
        in_specs=(P(None, "tm"), P(), P(None, "tm", "tile", None), P("tile", None)),
        out_specs=(P("tm", "tile", None), P("tm", "tile", None)),
        check_vma=False,
    )
```

```python
import functools
import math

import jax
import jax.numpy as jnp
from jax import lax
from jax.experimental import pallas as pl
from jax.experimental.pallas import tpu as pltpu
from jax.sharding import PartitionSpec as P

F32 = jnp.float32
BF16 = jnp.bfloat16
VMEM = pltpu.VMEM
DAY_GROUPS = (32, 24, 8)
SUB_DAYS = 8
GROUP = 32
LON_BLOCK = 512
BLOCK_DAYS = 16
VMEM_LIMIT = 40 << 20


def iota(shape, dim):
    return lax.broadcasted_iota(jnp.int32, shape, dim)


def after(value, *earlier):
    return lax.optimization_barrier((value, *earlier))[0]


def spread(comp, lat):
    share = comp.shape[1]
    shape = (share, share * lat)
    rep = jnp.where(iota(shape, 1) // lat == iota(shape, 0), 1.0, 0.0).astype(BF16)
    return jnp.dot(comp, rep, preferred_element_type=F32)


def only_row(wide, row, lat):
    return jnp.where(iota(wide.shape, 1) % lat == row, wide, 0.0).astype(BF16)


def components_kernel(place, *refs):
    pcs_refs, (st_ref, comp_ref, all_ref) = refs[:-3], refs[-3:]
    pairs, lags, _ = st_ref.shape
    day_dev = pcs_refs[0].shape[1]
    days = day_dev * len(pcs_refs)
    share = comp_ref.shape[1] // len(pcs_refs)
    count = comp_ref.shape[0] // 2
    lane_owner = iota((pairs, days), 1) // day_dev
    series = jnp.zeros((pairs, days), F32)
    for other, ref in enumerate(pcs_refs):
        tiled = jnp.concatenate([ref[...]] * len(pcs_refs), axis=1)
        series = jnp.where(lane_owner == place[2] ^ other, tiled, series)
    window = jnp.minimum(iota((days, share), 0) + 1, lags).astype(F32)
    lagged = []
    for k in range(pairs):
        row = jnp.concatenate([jnp.zeros((1, 128), F32), series[k:k + 1], jnp.zeros((1, 128), F32)], axis=1)
        wide = jnp.broadcast_to(row, (lags, days + 256))
        shifted = pltpu.roll(wide, 0, 1, stride=1, stride_axis=0)
        lagged.append(shifted[:, 128:128 + days].T)
    for half in range(len(pcs_refs)):
        first = pl.multiple_of((place[2] ^ half) * share, share)
        total = jnp.zeros((days, share), F32)
        for k in range(pairs):
            total += jnp.dot(lagged[k], st_ref[k, :, pl.ds(first, share)], precision=lax.Precision.HIGHEST, preferred_element_type=F32)
        all_ref[...] = total / window
        for side in range(2):
            rows = all_ref[pl.ds(pl.multiple_of(place[side], count), count), :].astype(BF16)
            comp_ref[side * count:(side + 1) * count, half * share:(half + 1) * share] = rows


def components_call(place, pcs_all, st_eof, share):
    day_dev = pcs_all[0].shape[1]
    return pl.pallas_call(
        components_kernel,
        in_specs=[pl.BlockSpec(memory_space=pltpu.SMEM)] + [pl.BlockSpec(memory_space=VMEM)] * (len(pcs_all) + 1),
        out_specs=pl.BlockSpec(memory_space=VMEM),
        out_shape=jax.ShapeDtypeStruct((2 * day_dev, len(pcs_all) * share), BF16),
        scratch_shapes=[VMEM((len(pcs_all) * day_dev, share), F32)],
        compiler_params=pltpu.CompilerParams(vmem_limit_bytes=12 << 20),
        cost_estimate=pl.CostEstimate(flops=0, bytes_accessed=128 << 20, transcendentals=0),
        name="components",
    )(place, *pcs_all, st_eof)


def pick_kernel(lat, *refs):
    groups, out_ref = refs[:-2], refs[-1]
    depth = groups[0].shape[1]
    chans = depth // lat
    row, col = iota((2 * chans, depth), 0), iota((2 * chans, depth), 1)
    wanted = (row % chans) * lat + (row // chans) * (lat - 1)
    pick = jnp.where(col == wanted, 1.0, 0.0).astype(BF16)
    for n, ref in enumerate(groups):
        found = jnp.dot(pick, ref[0], preferred_element_type=F32).astype(BF16)
        for end in range(2):
            out_ref[end, n * chans:(n + 1) * chans, :] = found[end * chans:(end + 1) * chans]


def pick_call(own, lat, x, token):
    _, depth, lon = own.shape
    share = depth // lat
    count = share // GROUP
    return pl.pallas_call(
        functools.partial(pick_kernel, lat),
        grid=(1,),
        in_specs=[pl.BlockSpec((1, GROUP * lat, lon), lambda i, n=n: (x, n, 0)) for n in range(count)]
        + [pl.BlockSpec(memory_space=pl.ANY)],
        out_specs=pl.BlockSpec((2, share, lon), lambda i: (0, 0, 0)),
        out_shape=jax.ShapeDtypeStruct((2, share, lon), BF16),
        compiler_params=pltpu.CompilerParams(vmem_limit_bytes=57 << 20),
        cost_estimate=pl.CostEstimate(flops=0, bytes_accessed=16 << 20, transcendentals=0),
        name="pick_end_rows",
    )(*[own] * count, token)


def edge_kernel(comp_ref, land_ref, *refs):
    parts, (low_ref, high_ref, ends_ref) = refs[:-3], refs[-3:]
    days = comp_ref.shape[0] // 2
    count = len(parts) // 2
    share = comp_ref.shape[1] // count
    lat = land_ref.shape[0]
    for x in range(2):
        for end in range(2):
            total = None
            for part in range(count):
                eof = parts[x * count + part][end]
                term = jnp.dot(comp_ref[:, part * share:(part + 1) * share], eof, preferred_element_type=F32)
                total = term if total is None else total + term
            at = end * (lat - 1)
            vel = (total * land_ref[at:at + 1, :].astype(F32)).astype(BF16)
            (high_ref, low_ref)[end][x] = vel[:days]
            ends_ref[x, end] = vel[days:]


def edge_call(comp, land, parts, block):
    days = comp.shape[0] // 2
    lat, lon = land.shape
    share = parts[0].shape[1]
    halo_spec = pl.BlockSpec((2, days, block), lambda n: (0, 0, n))
    halo_shape = jax.ShapeDtypeStruct((2, days, lon), BF16)
    return pl.pallas_call(
        edge_kernel,
        grid=(lon // block,),
        in_specs=[pl.BlockSpec(comp.shape, lambda n: (0, 0)), pl.BlockSpec((lat, block), lambda n: (0, n))]
        + [pl.BlockSpec((2, share, block), lambda n: (0, 0, n))] * len(parts),
        out_specs=[halo_spec, halo_spec, pl.BlockSpec((2, 2, days, block), lambda n: (0, 0, 0, n))],
        out_shape=[halo_shape, halo_shape, jax.ShapeDtypeStruct((2, 2, days, lon), BF16)],
        compiler_params=pltpu.CompilerParams(vmem_limit_bytes=24 << 20),
        name="end_rows",
    )(comp, land, *parts)


def inner_kernel(lat, first, span, comp_ref, own_ref, oth_ref, send_ref, keep_ref, x_ref):
    days = comp_ref.shape[0]
    depth = own_ref.shape[1]
    share = depth // lat
    cut = send_ref.shape[1]

    @pl.when((pl.program_id(0) == 0) & (pl.program_id(1) == 0))
    def _():
        for half in range(2):
            chan = slice(half * share, (half + 1) * share)
            cols = slice(half * depth, (half + 1) * depth)
            wide = spread(comp_ref[first:first + span, chan], lat)
            tall = []
            for day in range(0, span, SUB_DAYS):
                tall += [only_row(wide[day:day + SUB_DAYS], row, lat) for row in range(1, lat - 1)]
            for at in range(0, len(tall), 2):
                x_ref[at * SUB_DAYS:(at + 2) * SUB_DAYS, cols] = jnp.concatenate(tall[at:at + 2], axis=0)
            wide = spread(comp_ref[days // 2 + first:days // 2 + first + span, chan], lat)
            shape = (span, lat, depth)
            tall = jnp.where(iota(shape, 2) % lat == iota(shape, 1), jnp.broadcast_to(wide[:, None, :], shape), 0.0)
            x_ref[cut:, cols] = tall.reshape(span * lat, depth).astype(BF16)

    acc = jnp.dot(x_ref[:, :depth], own_ref[0], preferred_element_type=F32)
    acc += jnp.dot(x_ref[:, depth:], oth_ref[0], preferred_element_type=F32)
    send_ref[0] = acc[:cut].astype(BF16)
    keep_ref[0] = acc[cut:]


def inner_call(comp, own, oth, lat, lon, first, span, block):
    depth = own.shape[1]
    rows = span * (2 * lat - 2)

    kinds = (((lat - 2) * span, BF16), (lat * span, F32))
    return pl.pallas_call(
        functools.partial(inner_kernel, lat, first, span),
        grid=(lon // block, 2),
        in_specs=[
            pl.BlockSpec(comp.shape, lambda n, x: (0, 0)),
            pl.BlockSpec((1, depth, block), lambda n, x: (x, 0, n)),
            pl.BlockSpec((1, depth, block), lambda n, x: (x, 0, n)),
        ],
        out_specs=[pl.BlockSpec((1, height, block), lambda n, x: (x, 0, n)) for height, _ in kinds],
        out_shape=[jax.ShapeDtypeStruct((2, height, lon), dtype) for height, dtype in kinds],
        scratch_shapes=[VMEM((rows, 2 * depth), BF16)],
        compiler_params=pltpu.CompilerParams(vmem_limit_bytes=VMEM_LIMIT),
        cost_estimate=pl.CostEstimate(flops=2 * rows * 2 * depth * 2 * lon, bytes_accessed=8 * depth * lon + 6 * lon * rows, transcendentals=0),
        name="inner_partials",
    )(comp, own, oth)


def select(shape, of_row, of_col):
    row, col = iota(shape, 0), iota(shape, 1)
    return jnp.where(of_row(row) == of_col(col), 1.0, 0.0).astype(BF16)


def curl_kernel(lat, first, keep_ref, inner_ref, low_ref, high_ref, ends_ref, land_ref, coef_ref, *rest):
    vort_ref, div_ref = rest[-2:]
    lon = land_ref.shape[1]
    chunk = SUB_DAYS
    rows = chunk * lat
    seen = low_ref.shape[1]
    skip = (first + pl.program_id(0) * chunk) % seen
    mask = land_ref[...].astype(F32)
    from_inner = select((rows, (lat - 2) * chunk), lambda r: (r % lat) * chunk + r // lat, lambda c: c + chunk)
    from_low = select((rows, seen), lambda r: (r % lat) * seen + r // lat + skip, lambda c: c)
    from_high = select((rows, seen), lambda r: (r % lat) * seen + r // lat + skip, lambda c: c + (lat - 1) * seen)
    row, col = iota((rows, rows), 0), iota((rows, rows), 1)
    up = jnp.where(row % lat < lat - 1, jnp.where(col == row + 1, 1.0, 0.0), 0.0).astype(BF16)
    down = jnp.where(row % lat > 0, jnp.where(col + 1 == row, 1.0, 0.0), 0.0).astype(BF16)
    dot = functools.partial(jnp.dot, preferred_element_type=F32)
    row = iota(mask.shape, 0)
    inner_mask = jnp.where((row > 0) & (row < lat - 1), mask, 0.0)[None]
    zonal, merid = [], []
    cos_up = coef_ref[0][None, :, :1]
    cos_down = coef_ref[1][None, :, :1]
    scale = coef_ref[2][None, :, :1] * mask[None]
    for x in range(2):
        total = keep_ref[x] + dot(from_inner, inner_ref[x])
        vel = (total.reshape(chunk, lat, lon) * inner_mask).astype(BF16).astype(F32).reshape(rows, lon)
        wide = vel + dot(from_low, ends_ref[x, 0]) + dot(from_high, ends_ref[x, 1])
        vel = wide.astype(BF16)
        above = dot(up, vel) + dot(from_high, high_ref[x])
        below = dot(down, vel) + dot(from_low, low_ref[x])
        zonal.append((pltpu.roll(wide, lon - 1, 1) - pltpu.roll(wide, 1, 1)).reshape(chunk, lat, lon))
        merid.append(cos_up * above.reshape(chunk, lat, lon) - cos_down * below.reshape(chunk, lat, lon))
    vort_ref[...] = (zonal[1] - merid[0]) * scale
    div_ref[...] = (zonal[0] + merid[1]) * scale


def curl_call(keep, inner, ends, halos, land, coef, outs, lat, days, first, span):
    lon = land.shape[1]
    per = BLOCK_DAYS // SUB_DAYS
    block = first // SUB_DAYS
    whole = lambda shape: pl.BlockSpec(shape, lambda i: (0,) * len(shape))
    out_spec = pl.BlockSpec((SUB_DAYS, lat, lon), lambda i: (block + i, 0, 0))
    return pl.pallas_call(
        functools.partial(curl_kernel, lat, first),
        grid=(span // SUB_DAYS,),
        in_specs=[
            pl.BlockSpec((2, lat * SUB_DAYS, lon), lambda i: (0, i, 0)),
            pl.BlockSpec((2, (lat - 2) * SUB_DAYS, lon), lambda i: (0, i, 0)),
        ]
        + [pl.BlockSpec((2, BLOCK_DAYS, lon), lambda i: (0, (block + i) // per, 0))] * 2
        + [pl.BlockSpec((2, 2, BLOCK_DAYS, lon), lambda i: (0, 0, (block + i) // per, 0))]
        + [whole(land.shape), whole(coef.shape)]
        + [pl.BlockSpec(memory_space=pl.ANY)] * len(outs),
        out_specs=[out_spec] * 2,
        out_shape=[jax.ShapeDtypeStruct((days, lat, lon), F32)] * 2,
        input_output_aliases={7: 0, 8: 1} if outs else {},
        compiler_params=pltpu.CompilerParams(vmem_limit_bytes=VMEM_LIMIT),
        cost_estimate=pl.CostEstimate(flops=20 * 2 * span * lat * lon, bytes_accessed=20 * span * lat * lon, transcendentals=0),
        name="curl_div",
    )(keep, inner, *halos, ends, land, coef, *outs)


def shards(pcs, st_eof, spatial_eof, land_sea):
    day_dev = pcs.shape[1]
    _, share, lat, lon = spatial_eof.shape
    depth = share * lat
    tm = lax.axis_index("tm")
    tiles = lax.axis_size("tile")
    tile = lax.axis_index("tile")
    swap_core = [(i, i ^ 1) for i in range(4)]
    swap_chip = [(i, i ^ 2) for i in range(4)]
    north = [(t * tiles + i, (t ^ 2) * tiles + i + 1) for t in range(4) for i in range(tiles - 1)]
    south = [(t * tiles + i + 1, (t ^ 2) * tiles + i) for t in range(4) for i in range(tiles - 1)]

    pcs_all = [pcs] + [lax.ppermute(pcs, "tm", [(i, i ^ s) for i in range(4)]) for s in (1, 2, 3)]
    own = spatial_eof.reshape(2, depth, lon)
    mine = [pick_call(own, lat, 0, pcs_all[1])]
    mine.append(pick_call(own, lat, 1, mine[0]))
    crossed = [lax.ppermute(after(m, *pcs_all[2:]), "tm", swap_chip) for m in mine]
    swapped = [lax.ppermute(m, "tm", swap_core) for m in mine]
    oth = lax.ppermute(after(own, pcs_all[1]), "tm", swap_core)

    place = jnp.stack([(tm ^ 2) * day_dev, tm * day_dev, tm]).astype(jnp.int32)
    comp = components_call(after(place, mine[1]), pcs_all, st_eof, share)

    inners, across = [], []
    first = 0
    for i, span in enumerate(DAY_GROUPS):
        send, keep = inner_call(comp, own, oth, lat, lon, first, span, LON_BLOCK)
        inners.append((lax.ppermute(send, "tm", swap_chip), keep))
        first += span
        if i < 2:
            across.append(lax.ppermute(after(crossed[i], send), "tm", swap_core))
            comp = after(comp, send, across[i])
        if i == 1:
            parts = [a for x in range(2) for a in (mine[x], swapped[x], crossed[x], across[x])]
            low, high, ends = edge_call(comp, land_sea, parts, LON_BLOCK)
            halos = [lax.ppermute(low, ("tm", "tile"), north), lax.ppermute(high, ("tm", "tile"), south)]
            comp = after(comp, low, inners[0][0])

    rows = (tile * lat).astype(F32) + jnp.arange(-1, lat + 1, dtype=F32)
    latitude = (-70.0 + 140.0 * (rows + 0.5) / (lat * tiles)) * (math.pi / 180.0)
    cosine = jnp.cos(latitude)
    coef = jnp.stack([cosine[2:], cosine[:-2], 0.5 / cosine[1:-1]])
    coef = jnp.broadcast_to(coef[:, :, None], (3, lat, 128))

    outs = []
    first = 0
    for span, (inner, keep) in zip(DAY_GROUPS, inners):
        outs = curl_call(keep, inner, ends, halos, land_sea, coef, outs, lat, day_dev, first, span)
        first += span
    return tuple(outs)


def solution(mesh):
    return jax.shard_map(
        shards,
        mesh=mesh,
        in_specs=(P(None, "tm"), P(), P(None, "tm", "tile", None), P("tile", None)),
        out_specs=(P("tm", "tile", None), P("tm", "tile", None)),
        check_vma=False,
    )
```

```python
import functools
import math

import jax
import jax.numpy as jnp
from jax import lax
from jax.experimental import pallas as pl
from jax.experimental.pallas import tpu as pltpu
from jax.sharding import PartitionSpec as P

F32 = jnp.float32
BF16 = jnp.bfloat16
VMEM = pltpu.VMEM
DAY_GROUPS = (32, 24, 8)
SUB_DAYS = 8
GROUP = 32
PICK_BLOCK = 1024
LON_BLOCK = 512
BLOCK_DAYS = 16
VMEM_LIMIT = 40 << 20


def iota(shape, dim):
    return lax.broadcasted_iota(jnp.int32, shape, dim)


def after(value, *earlier):
    return lax.optimization_barrier((value, *earlier))[0]


def spread(comp, lat):
    share = comp.shape[1]
    shape = (share, share * lat)
    rep = jnp.where(iota(shape, 1) // lat == iota(shape, 0), 1.0, 0.0).astype(BF16)
    return jnp.dot(comp, rep, preferred_element_type=F32)


def only_row(wide, row, lat):
    return jnp.where(iota(wide.shape, 1) % lat == row, wide, 0.0).astype(BF16)


def components_kernel(place, *refs):
    pcs_refs, (st_ref, comp_ref, all_ref) = refs[:-3], refs[-3:]
    pairs, lags, _ = st_ref.shape
    day_dev = pcs_refs[0].shape[1]
    days = day_dev * len(pcs_refs)
    share = comp_ref.shape[1] // len(pcs_refs)
    count = comp_ref.shape[0] // 2
    lane_owner = iota((pairs, days), 1) // day_dev
    series = jnp.zeros((pairs, days), F32)
    for other, ref in enumerate(pcs_refs):
        tiled = jnp.concatenate([ref[...]] * len(pcs_refs), axis=1)
        series = jnp.where(lane_owner == place[2] ^ other, tiled, series)
    window = jnp.minimum(iota((days, share), 0) + 1, lags).astype(F32)
    lagged = []
    for k in range(pairs):
        row = jnp.concatenate([jnp.zeros((1, 128), F32), series[k:k + 1], jnp.zeros((1, 128), F32)], axis=1)
        wide = jnp.broadcast_to(row, (lags, days + 256))
        shifted = pltpu.roll(wide, 0, 1, stride=1, stride_axis=0)
        lagged.append(shifted[:, 128:128 + days].T)
    for half in range(len(pcs_refs)):
        first = pl.multiple_of((place[2] ^ half) * share, share)
        total = jnp.zeros((days, share), F32)
        for k in range(pairs):
            total += jnp.dot(lagged[k], st_ref[k, :, pl.ds(first, share)], precision=lax.Precision.HIGHEST, preferred_element_type=F32)
        all_ref[...] = total / window
        for side in range(2):
            rows = all_ref[pl.ds(pl.multiple_of(place[side], count), count), :].astype(BF16)
            comp_ref[side * count:(side + 1) * count, half * share:(half + 1) * share] = rows


def components_call(place, pcs_all, st_eof, share):
    day_dev = pcs_all[0].shape[1]
    return pl.pallas_call(
        components_kernel,
        in_specs=[pl.BlockSpec(memory_space=pltpu.SMEM)] + [pl.BlockSpec(memory_space=VMEM)] * (len(pcs_all) + 1),
        out_specs=pl.BlockSpec(memory_space=VMEM),
        out_shape=jax.ShapeDtypeStruct((2 * day_dev, len(pcs_all) * share), BF16),
        scratch_shapes=[VMEM((len(pcs_all) * day_dev, share), F32)],
        compiler_params=pltpu.CompilerParams(vmem_limit_bytes=12 << 20),
        cost_estimate=pl.CostEstimate(flops=0, bytes_accessed=128 << 20, transcendentals=0),
        name="components",
    )(place, *pcs_all, st_eof)


def pick_kernel(lat, *refs):
    groups, out_ref = refs[:-2], refs[-1]
    depth = groups[0].shape[1]
    chans = depth // lat
    row, col = iota((2 * chans, depth), 0), iota((2 * chans, depth), 1)
    wanted = (row % chans) * lat + (row // chans) * (lat - 1)
    pick = jnp.where(col == wanted, 1.0, 0.0).astype(BF16)
    for n, ref in enumerate(groups):
        found = jnp.dot(pick, ref[0], preferred_element_type=F32).astype(BF16)
        for end in range(2):
            out_ref[end, n * chans:(n + 1) * chans, :] = found[end * chans:(end + 1) * chans]


def pick_call(own, lat, x, token):
    _, depth, lon = own.shape
    share = depth // lat
    count = share // GROUP
    return pl.pallas_call(
        functools.partial(pick_kernel, lat),
        grid=(lon // PICK_BLOCK,),
        in_specs=[pl.BlockSpec((1, GROUP * lat, PICK_BLOCK), lambda i, n=n: (x, n, i)) for n in range(count)]
        + [pl.BlockSpec(memory_space=pl.ANY)],
        out_specs=pl.BlockSpec((2, share, PICK_BLOCK), lambda i: (0, 0, i)),
        out_shape=jax.ShapeDtypeStruct((2, share, lon), BF16),
        compiler_params=pltpu.CompilerParams(vmem_limit_bytes=57 << 20),
        cost_estimate=pl.CostEstimate(flops=0, bytes_accessed=16 << 20, transcendentals=0),
        name="pick_end_rows",
    )(*[own] * count, token)


def edge_kernel(comp_ref, land_ref, *refs):
    parts, (low_ref, high_ref, ends_ref) = refs[:-3], refs[-3:]
    days = comp_ref.shape[0] // 2
    count = len(parts) // 2
    share = comp_ref.shape[1] // count
    lat = land_ref.shape[0]
    for x in range(2):
        for end in range(2):
            total = None
            for part in range(count):
                eof = parts[x * count + part][end]
                term = jnp.dot(comp_ref[:, part * share:(part + 1) * share], eof, preferred_element_type=F32)
                total = term if total is None else total + term
            at = end * (lat - 1)
            vel = (total * land_ref[at:at + 1, :].astype(F32)).astype(BF16)
            (high_ref, low_ref)[end][x] = vel[:days]
            ends_ref[x, end] = vel[days:]


def edge_call(comp, land, parts, block):
    days = comp.shape[0] // 2
    lat, lon = land.shape
    share = parts[0].shape[1]
    halo_spec = pl.BlockSpec((2, days, block), lambda n: (0, 0, n))
    halo_shape = jax.ShapeDtypeStruct((2, days, lon), BF16)
    return pl.pallas_call(
        edge_kernel,
        grid=(lon // block,),
        in_specs=[pl.BlockSpec(comp.shape, lambda n: (0, 0)), pl.BlockSpec((lat, block), lambda n: (0, n))]
        + [pl.BlockSpec((2, share, block), lambda n: (0, 0, n))] * len(parts),
        out_specs=[halo_spec, halo_spec, pl.BlockSpec((2, 2, days, block), lambda n: (0, 0, 0, n))],
        out_shape=[halo_shape, halo_shape, jax.ShapeDtypeStruct((2, 2, days, lon), BF16)],
        compiler_params=pltpu.CompilerParams(vmem_limit_bytes=24 << 20),
        name="end_rows",
    )(comp, land, *parts)


def inner_kernel(lat, first, span, comp_ref, own_ref, oth_ref, send_ref, keep_ref, x_ref):
    days = comp_ref.shape[0]
    depth = own_ref.shape[1]
    share = depth // lat
    cut = send_ref.shape[1]

    @pl.when((pl.program_id(0) == 0) & (pl.program_id(1) == 0))
    def _():
        for half in range(2):
            chan = slice(half * share, (half + 1) * share)
            cols = slice(half * depth, (half + 1) * depth)
            wide = spread(comp_ref[first:first + span, chan], lat)
            tall = []
            for day in range(0, span, SUB_DAYS):
                tall += [only_row(wide[day:day + SUB_DAYS], row, lat) for row in range(1, lat - 1)]
            for at in range(0, len(tall), 2):
                x_ref[at * SUB_DAYS:(at + 2) * SUB_DAYS, cols] = jnp.concatenate(tall[at:at + 2], axis=0)
            wide = spread(comp_ref[days // 2 + first:days // 2 + first + span, chan], lat)
            shape = (span, lat, depth)
            tall = jnp.where(iota(shape, 2) % lat == iota(shape, 1), jnp.broadcast_to(wide[:, None, :], shape), 0.0)
            x_ref[cut:, cols] = tall.reshape(span * lat, depth).astype(BF16)

    acc = jnp.dot(x_ref[:, :depth], own_ref[0], preferred_element_type=F32)
    acc += jnp.dot(x_ref[:, depth:], oth_ref[0], preferred_element_type=F32)
    send_ref[0] = acc[:cut].astype(BF16)
    keep_ref[0] = acc[cut:]


def inner_call(comp, own, oth, lat, lon, first, span, block):
    depth = own.shape[1]
    rows = span * (2 * lat - 2)

    kinds = (((lat - 2) * span, BF16), (lat * span, F32))
    return pl.pallas_call(
        functools.partial(inner_kernel, lat, first, span),
        grid=(lon // block, 2),
        in_specs=[
            pl.BlockSpec(comp.shape, lambda n, x: (0, 0)),
            pl.BlockSpec((1, depth, block), lambda n, x: (x, 0, n)),
            pl.BlockSpec((1, depth, block), lambda n, x: (x, 0, n)),
        ],
        out_specs=[pl.BlockSpec((1, height, block), lambda n, x: (x, 0, n)) for height, _ in kinds],
        out_shape=[jax.ShapeDtypeStruct((2, height, lon), dtype) for height, dtype in kinds],
        scratch_shapes=[VMEM((rows, 2 * depth), BF16)],
        compiler_params=pltpu.CompilerParams(vmem_limit_bytes=VMEM_LIMIT),
        cost_estimate=pl.CostEstimate(flops=2 * rows * 2 * depth * 2 * lon, bytes_accessed=8 * depth * lon + 6 * lon * rows, transcendentals=0),
        name="inner_partials",
    )(comp, own, oth)


def select(shape, of_row, of_col):
    row, col = iota(shape, 0), iota(shape, 1)
    return jnp.where(of_row(row) == of_col(col), 1.0, 0.0).astype(BF16)


def curl_kernel(lat, first, keep_ref, inner_ref, low_ref, high_ref, ends_ref, land_ref, coef_ref, *rest):
    vort_ref, div_ref = rest[-2:]
    lon = land_ref.shape[1]
    chunk = SUB_DAYS
    rows = chunk * lat
    seen = low_ref.shape[1]
    skip = (first + pl.program_id(0) * chunk) % seen
    mask = land_ref[...].astype(F32)
    from_inner = select((rows, (lat - 2) * chunk), lambda r: (r % lat) * chunk + r // lat, lambda c: c + chunk)
    from_low = select((rows, seen), lambda r: (r % lat) * seen + r // lat + skip, lambda c: c)
    from_high = select((rows, seen), lambda r: (r % lat) * seen + r // lat + skip, lambda c: c + (lat - 1) * seen)
    row, col = iota((rows, rows), 0), iota((rows, rows), 1)
    up = jnp.where(row % lat < lat - 1, jnp.where(col == row + 1, 1.0, 0.0), 0.0).astype(BF16)
    down = jnp.where(row % lat > 0, jnp.where(col + 1 == row, 1.0, 0.0), 0.0).astype(BF16)
    dot = functools.partial(jnp.dot, preferred_element_type=F32)
    row = iota(mask.shape, 0)
    inner_mask = jnp.where((row > 0) & (row < lat - 1), mask, 0.0)[None]
    zonal, merid = [], []
    cos_up = coef_ref[0][None, :, :1]
    cos_down = coef_ref[1][None, :, :1]
    scale = coef_ref[2][None, :, :1] * mask[None]
    for x in range(2):
        total = keep_ref[x] + dot(from_inner, inner_ref[x])
        vel = (total.reshape(chunk, lat, lon) * inner_mask).astype(BF16).astype(F32).reshape(rows, lon)
        wide = vel + dot(from_low, ends_ref[x, 0]) + dot(from_high, ends_ref[x, 1])
        vel = wide.astype(BF16)
        above = dot(up, vel) + dot(from_high, high_ref[x])
        below = dot(down, vel) + dot(from_low, low_ref[x])
        zonal.append((pltpu.roll(wide, lon - 1, 1) - pltpu.roll(wide, 1, 1)).reshape(chunk, lat, lon))
        merid.append(cos_up * above.reshape(chunk, lat, lon) - cos_down * below.reshape(chunk, lat, lon))
    vort_ref[...] = (zonal[1] - merid[0]) * scale
    div_ref[...] = (zonal[0] + merid[1]) * scale


def curl_call(keep, inner, ends, halos, land, coef, outs, lat, days, first, span):
    lon = land.shape[1]
    per = BLOCK_DAYS // SUB_DAYS
    block = first // SUB_DAYS
    whole = lambda shape: pl.BlockSpec(shape, lambda i: (0,) * len(shape))
    out_spec = pl.BlockSpec((SUB_DAYS, lat, lon), lambda i: (block + i, 0, 0))
    return pl.pallas_call(
        functools.partial(curl_kernel, lat, first),
        grid=(span // SUB_DAYS,),
        in_specs=[
            pl.BlockSpec((2, lat * SUB_DAYS, lon), lambda i: (0, i, 0)),
            pl.BlockSpec((2, (lat - 2) * SUB_DAYS, lon), lambda i: (0, i, 0)),
        ]
        + [pl.BlockSpec((2, BLOCK_DAYS, lon), lambda i: (0, (block + i) // per, 0))] * 2
        + [pl.BlockSpec((2, 2, BLOCK_DAYS, lon), lambda i: (0, 0, (block + i) // per, 0))]
        + [whole(land.shape), whole(coef.shape)]
        + [pl.BlockSpec(memory_space=pl.ANY)] * len(outs),
        out_specs=[out_spec] * 2,
        out_shape=[jax.ShapeDtypeStruct((days, lat, lon), F32)] * 2,
        input_output_aliases={7: 0, 8: 1} if outs else {},
        compiler_params=pltpu.CompilerParams(vmem_limit_bytes=VMEM_LIMIT),
        cost_estimate=pl.CostEstimate(flops=20 * 2 * span * lat * lon, bytes_accessed=20 * span * lat * lon, transcendentals=0),
        name="curl_div",
    )(keep, inner, *halos, ends, land, coef, *outs)


def shards(pcs, st_eof, spatial_eof, land_sea):
    day_dev = pcs.shape[1]
    _, share, lat, lon = spatial_eof.shape
    depth = share * lat
    tm = lax.axis_index("tm")
    tiles = lax.axis_size("tile")
    tile = lax.axis_index("tile")
    swap_core = [(i, i ^ 1) for i in range(4)]
    swap_chip = [(i, i ^ 2) for i in range(4)]
    north = [(t * tiles + i, (t ^ 2) * tiles + i + 1) for t in range(4) for i in range(tiles - 1)]
    south = [(t * tiles + i + 1, (t ^ 2) * tiles + i) for t in range(4) for i in range(tiles - 1)]

    pcs_all = [pcs] + [lax.ppermute(pcs, "tm", [(i, i ^ s) for i in range(4)]) for s in (1, 2, 3)]
    own = spatial_eof.reshape(2, depth, lon)
    mine = [pick_call(own, lat, 0, pcs_all[1])]
    mine.append(pick_call(own, lat, 1, mine[0]))
    crossed = [lax.ppermute(after(m, *pcs_all[2:]), "tm", swap_chip) for m in mine]
    swapped = [lax.ppermute(m, "tm", swap_core) for m in mine]
    oth = lax.ppermute(after(own, pcs_all[1]), "tm", swap_core)

    place = jnp.stack([(tm ^ 2) * day_dev, tm * day_dev, tm]).astype(jnp.int32)
    comp = components_call(after(place, mine[1]), pcs_all, st_eof, share)

    inners, across = [], []
    first = 0
    for i, span in enumerate(DAY_GROUPS):
        send, keep = inner_call(comp, own, oth, lat, lon, first, span, LON_BLOCK)
        inners.append((lax.ppermute(send, "tm", swap_chip), keep))
        first += span
        if i < 2:
            across.append(lax.ppermute(after(crossed[i], send), "tm", swap_core))
            comp = after(comp, send, across[i])
        if i == 1:
            parts = [a for x in range(2) for a in (mine[x], swapped[x], crossed[x], across[x])]
            low, high, ends = edge_call(comp, land_sea, parts, LON_BLOCK)
            halos = [lax.ppermute(low, ("tm", "tile"), north), lax.ppermute(high, ("tm", "tile"), south)]
            comp = after(comp, low, inners[0][0])

    rows = (tile * lat).astype(F32) + jnp.arange(-1, lat + 1, dtype=F32)
    latitude = (-70.0 + 140.0 * (rows + 0.5) / (lat * tiles)) * (math.pi / 180.0)
    cosine = jnp.cos(latitude)
    coef = jnp.stack([cosine[2:], cosine[:-2], 0.5 / cosine[1:-1]])
    coef = jnp.broadcast_to(coef[:, :, None], (3, lat, 128))

    outs = []
    first = 0
    for span, (inner, keep) in zip(DAY_GROUPS, inners):
        outs = curl_call(keep, inner, ends, halos, land_sea, coef, outs, lat, day_dev, first, span)
        first += span
    return tuple(outs)


def solution(mesh):
    return jax.shard_map(
        shards,
        mesh=mesh,
        in_specs=(P(None, "tm"), P(), P(None, "tm", "tile", None), P("tile", None)),
        out_specs=(P("tm", "tile", None), P("tm", "tile", None)),
        check_vma=False,
    )
```

```python
import functools
import math

import jax
import jax.numpy as jnp
from jax import lax
from jax.experimental import pallas as pl
from jax.experimental.pallas import tpu as pltpu
from jax.sharding import PartitionSpec as P

F32 = jnp.float32
BF16 = jnp.bfloat16
VMEM = pltpu.VMEM
DAY_GROUPS = (24, 32, 8)
SUB_DAYS = 8
GROUP = 32
PICK_BLOCK = 1024
LON_BLOCK = 512
BLOCK_DAYS = 16
VMEM_LIMIT = 40 << 20


def iota(shape, dim):
    return lax.broadcasted_iota(jnp.int32, shape, dim)


def after(value, *earlier):
    return lax.optimization_barrier((value, *earlier))[0]


def spread(comp, lat):
    share = comp.shape[1]
    shape = (share, share * lat)
    rep = jnp.where(iota(shape, 1) // lat == iota(shape, 0), 1.0, 0.0).astype(BF16)
    return jnp.dot(comp, rep, preferred_element_type=F32)


def only_row(wide, row, lat):
    return jnp.where(iota(wide.shape, 1) % lat == row, wide, 0.0).astype(BF16)


def components_kernel(place, *refs):
    pcs_refs, (st_ref, comp_ref, all_ref) = refs[:-3], refs[-3:]
    pairs, lags, _ = st_ref.shape
    day_dev = pcs_refs[0].shape[1]
    days = day_dev * len(pcs_refs)
    share = comp_ref.shape[1] // len(pcs_refs)
    count = comp_ref.shape[0] // 2
    lane_owner = iota((pairs, days), 1) // day_dev
    series = jnp.zeros((pairs, days), F32)
    for other, ref in enumerate(pcs_refs):
        tiled = jnp.concatenate([ref[...]] * len(pcs_refs), axis=1)
        series = jnp.where(lane_owner == place[2] ^ other, tiled, series)
    window = jnp.minimum(iota((days, share), 0) + 1, lags).astype(F32)
    lagged = []
    for k in range(pairs):
        row = jnp.concatenate([jnp.zeros((1, 128), F32), series[k:k + 1], jnp.zeros((1, 128), F32)], axis=1)
        wide = jnp.broadcast_to(row, (lags, days + 256))
        shifted = pltpu.roll(wide, 0, 1, stride=1, stride_axis=0)
        lagged.append(shifted[:, 128:128 + days].T)
    for half in range(len(pcs_refs)):
        first = pl.multiple_of((place[2] ^ half) * share, share)
        total = jnp.zeros((days, share), F32)
        for k in range(pairs):
            total += jnp.dot(lagged[k], st_ref[k, :, pl.ds(first, share)], precision=lax.Precision.HIGHEST, preferred_element_type=F32)
        all_ref[...] = total / window
        for side in range(2):
            rows = all_ref[pl.ds(pl.multiple_of(place[side], count), count), :].astype(BF16)
            comp_ref[side * count:(side + 1) * count, half * share:(half + 1) * share] = rows


def components_call(place, pcs_all, st_eof, share):
    day_dev = pcs_all[0].shape[1]
    return pl.pallas_call(
        components_kernel,
        in_specs=[pl.BlockSpec(memory_space=pltpu.SMEM)] + [pl.BlockSpec(memory_space=VMEM)] * (len(pcs_all) + 1),
        out_specs=pl.BlockSpec(memory_space=VMEM),
        out_shape=jax.ShapeDtypeStruct((2 * day_dev, len(pcs_all) * share), BF16),
        scratch_shapes=[VMEM((len(pcs_all) * day_dev, share), F32)],
        compiler_params=pltpu.CompilerParams(vmem_limit_bytes=12 << 20),
        cost_estimate=pl.CostEstimate(flops=0, bytes_accessed=128 << 20, transcendentals=0),
        name="components",
    )(place, *pcs_all, st_eof)


def pick_kernel(lat, *refs):
    groups, out_ref = refs[:-2], refs[-1]
    depth = groups[0].shape[1]
    chans = depth // lat
    row, col = iota((2 * chans, depth), 0), iota((2 * chans, depth), 1)
    wanted = (row % chans) * lat + (row // chans) * (lat - 1)
    pick = jnp.where(col == wanted, 1.0, 0.0).astype(BF16)
    for n, ref in enumerate(groups):
        found = jnp.dot(pick, ref[0], preferred_element_type=F32).astype(BF16)
        for end in range(2):
            out_ref[end, n * chans:(n + 1) * chans, :] = found[end * chans:(end + 1) * chans]


def pick_call(own, lat, x, token):
    _, depth, lon = own.shape
    share = depth // lat
    count = share // GROUP
    return pl.pallas_call(
        functools.partial(pick_kernel, lat),
        grid=(lon // PICK_BLOCK,),
        in_specs=[pl.BlockSpec((1, GROUP * lat, PICK_BLOCK), lambda i, n=n: (x, n, i)) for n in range(count)]
        + [pl.BlockSpec(memory_space=pl.ANY)],
        out_specs=pl.BlockSpec((2, share, PICK_BLOCK), lambda i: (0, 0, i)),
        out_shape=jax.ShapeDtypeStruct((2, share, lon), BF16),
        compiler_params=pltpu.CompilerParams(vmem_limit_bytes=57 << 20),
        cost_estimate=pl.CostEstimate(flops=0, bytes_accessed=16 << 20, transcendentals=0),
        name="pick_end_rows",
    )(*[own] * count, token)


def edge_kernel(comp_ref, land_ref, *refs):
    parts, (low_ref, high_ref, ends_ref) = refs[:-3], refs[-3:]
    days = comp_ref.shape[0] // 2
    count = len(parts) // 2
    share = comp_ref.shape[1] // count
    lat = land_ref.shape[0]
    for x in range(2):
        for end in range(2):
            total = None
            for part in range(count):
                eof = parts[x * count + part][end]
                term = jnp.dot(comp_ref[:, part * share:(part + 1) * share], eof, preferred_element_type=F32)
                total = term if total is None else total + term
            at = end * (lat - 1)
            vel = (total * land_ref[at:at + 1, :].astype(F32)).astype(BF16)
            (high_ref, low_ref)[end][x] = vel[:days]
            ends_ref[x, end] = vel[days:]


def edge_call(comp, land, parts, block):
    days = comp.shape[0] // 2
    lat, lon = land.shape
    share = parts[0].shape[1]
    halo_spec = pl.BlockSpec((2, days, block), lambda n: (0, 0, n))
    halo_shape = jax.ShapeDtypeStruct((2, days, lon), BF16)
    return pl.pallas_call(
        edge_kernel,
        grid=(lon // block,),
        in_specs=[pl.BlockSpec(comp.shape, lambda n: (0, 0)), pl.BlockSpec((lat, block), lambda n: (0, n))]
        + [pl.BlockSpec((2, share, block), lambda n: (0, 0, n))] * len(parts),
        out_specs=[halo_spec, halo_spec, pl.BlockSpec((2, 2, days, block), lambda n: (0, 0, 0, n))],
        out_shape=[halo_shape, halo_shape, jax.ShapeDtypeStruct((2, 2, days, lon), BF16)],
        compiler_params=pltpu.CompilerParams(vmem_limit_bytes=24 << 20),
        name="end_rows",
    )(comp, land, *parts)


def inner_kernel(lat, first, span, comp_ref, own_ref, oth_ref, send_ref, keep_ref, x_ref):
    days = comp_ref.shape[0]
    depth = own_ref.shape[1]
    share = depth // lat
    cut = send_ref.shape[1]

    @pl.when((pl.program_id(0) == 0) & (pl.program_id(1) == 0))
    def _():
        for half in range(2):
            chan = slice(half * share, (half + 1) * share)
            cols = slice(half * depth, (half + 1) * depth)
            wide = spread(comp_ref[first:first + span, chan], lat)
            tall = []
            for day in range(0, span, SUB_DAYS):
                tall += [only_row(wide[day:day + SUB_DAYS], row, lat) for row in range(1, lat - 1)]
            for at in range(0, len(tall), 2):
                x_ref[at * SUB_DAYS:(at + 2) * SUB_DAYS, cols] = jnp.concatenate(tall[at:at + 2], axis=0)
            wide = spread(comp_ref[days // 2 + first:days // 2 + first + span, chan], lat)
            shape = (span, lat, depth)
            tall = jnp.where(iota(shape, 2) % lat == iota(shape, 1), jnp.broadcast_to(wide[:, None, :], shape), 0.0)
            x_ref[cut:, cols] = tall.reshape(span * lat, depth).astype(BF16)

    acc = jnp.dot(x_ref[:, :depth], own_ref[0], preferred_element_type=F32)
    acc += jnp.dot(x_ref[:, depth:], oth_ref[0], preferred_element_type=F32)
    send_ref[0] = acc[:cut].astype(BF16)
    keep_ref[0] = acc[cut:]


def inner_call(comp, own, oth, lat, lon, first, span, block):
    depth = own.shape[1]
    rows = span * (2 * lat - 2)

    kinds = (((lat - 2) * span, BF16), (lat * span, F32))
    return pl.pallas_call(
        functools.partial(inner_kernel, lat, first, span),
        grid=(lon // block, 2),
        in_specs=[
            pl.BlockSpec(comp.shape, lambda n, x: (0, 0)),
            pl.BlockSpec((1, depth, block), lambda n, x: (x, 0, n)),
            pl.BlockSpec((1, depth, block), lambda n, x: (x, 0, n)),
        ],
        out_specs=[pl.BlockSpec((1, height, block), lambda n, x: (x, 0, n)) for height, _ in kinds],
        out_shape=[jax.ShapeDtypeStruct((2, height, lon), dtype) for height, dtype in kinds],
        scratch_shapes=[VMEM((rows, 2 * depth), BF16)],
        compiler_params=pltpu.CompilerParams(vmem_limit_bytes=VMEM_LIMIT),
        cost_estimate=pl.CostEstimate(flops=2 * rows * 2 * depth * 2 * lon, bytes_accessed=8 * depth * lon + 6 * lon * rows, transcendentals=0),
        name="inner_partials",
    )(comp, own, oth)


def select(shape, of_row, of_col):
    row, col = iota(shape, 0), iota(shape, 1)
    return jnp.where(of_row(row) == of_col(col), 1.0, 0.0).astype(BF16)


def curl_kernel(lat, first, keep_ref, inner_ref, low_ref, high_ref, ends_ref, land_ref, coef_ref, *rest):
    vort_ref, div_ref = rest[-2:]
    lon = land_ref.shape[1]
    chunk = SUB_DAYS
    rows = chunk * lat
    seen = low_ref.shape[1]
    skip = (first + pl.program_id(0) * chunk) % seen
    mask = land_ref[...].astype(F32)
    from_inner = select((rows, (lat - 2) * chunk), lambda r: (r % lat) * chunk + r // lat, lambda c: c + chunk)
    from_low = select((rows, seen), lambda r: (r % lat) * seen + r // lat + skip, lambda c: c)
    from_high = select((rows, seen), lambda r: (r % lat) * seen + r // lat + skip, lambda c: c + (lat - 1) * seen)
    row, col = iota((rows, rows), 0), iota((rows, rows), 1)
    up = jnp.where(row % lat < lat - 1, jnp.where(col == row + 1, 1.0, 0.0), 0.0).astype(BF16)
    down = jnp.where(row % lat > 0, jnp.where(col + 1 == row, 1.0, 0.0), 0.0).astype(BF16)
    dot = functools.partial(jnp.dot, preferred_element_type=F32)
    row = iota(mask.shape, 0)
    inner_mask = jnp.where((row > 0) & (row < lat - 1), mask, 0.0)[None]
    zonal, merid = [], []
    cos_up = coef_ref[0][None, :, :1]
    cos_down = coef_ref[1][None, :, :1]
    scale = coef_ref[2][None, :, :1] * mask[None]
    for x in range(2):
        total = keep_ref[x] + dot(from_inner, inner_ref[x])
        vel = (total.reshape(chunk, lat, lon) * inner_mask).astype(BF16).astype(F32).reshape(rows, lon)
        wide = vel + dot(from_low, ends_ref[x, 0]) + dot(from_high, ends_ref[x, 1])
        vel = wide.astype(BF16)
        above = dot(up, vel) + dot(from_high, high_ref[x])
        below = dot(down, vel) + dot(from_low, low_ref[x])
        zonal.append((pltpu.roll(wide, lon - 1, 1) - pltpu.roll(wide, 1, 1)).reshape(chunk, lat, lon))
        merid.append(cos_up * above.reshape(chunk, lat, lon) - cos_down * below.reshape(chunk, lat, lon))
    vort_ref[...] = (zonal[1] - merid[0]) * scale
    div_ref[...] = (zonal[0] + merid[1]) * scale


def curl_call(keep, inner, ends, halos, land, coef, outs, lat, days, first, span):
    lon = land.shape[1]
    per = BLOCK_DAYS // SUB_DAYS
    block = first // SUB_DAYS
    whole = lambda shape: pl.BlockSpec(shape, lambda i: (0,) * len(shape))
    out_spec = pl.BlockSpec((SUB_DAYS, lat, lon), lambda i: (block + i, 0, 0))
    return pl.pallas_call(
        functools.partial(curl_kernel, lat, first),
        grid=(span // SUB_DAYS,),
        in_specs=[
            pl.BlockSpec((2, lat * SUB_DAYS, lon), lambda i: (0, i, 0)),
            pl.BlockSpec((2, (lat - 2) * SUB_DAYS, lon), lambda i: (0, i, 0)),
        ]
        + [pl.BlockSpec((2, BLOCK_DAYS, lon), lambda i: (0, (block + i) // per, 0))] * 2
        + [pl.BlockSpec((2, 2, BLOCK_DAYS, lon), lambda i: (0, 0, (block + i) // per, 0))]
        + [whole(land.shape), whole(coef.shape)]
        + [pl.BlockSpec(memory_space=pl.ANY)] * len(outs),
        out_specs=[out_spec] * 2,
        out_shape=[jax.ShapeDtypeStruct((days, lat, lon), F32)] * 2,
        input_output_aliases={7: 0, 8: 1} if outs else {},
        compiler_params=pltpu.CompilerParams(vmem_limit_bytes=VMEM_LIMIT),
        cost_estimate=pl.CostEstimate(flops=20 * 2 * span * lat * lon, bytes_accessed=20 * span * lat * lon, transcendentals=0),
        name="curl_div",
    )(keep, inner, *halos, ends, land, coef, *outs)


def shards(pcs, st_eof, spatial_eof, land_sea):
    day_dev = pcs.shape[1]
    _, share, lat, lon = spatial_eof.shape
    depth = share * lat
    tm = lax.axis_index("tm")
    tiles = lax.axis_size("tile")
    tile = lax.axis_index("tile")
    swap_core = [(i, i ^ 1) for i in range(4)]
    swap_chip = [(i, i ^ 2) for i in range(4)]
    north = [(t * tiles + i, (t ^ 2) * tiles + i + 1) for t in range(4) for i in range(tiles - 1)]
    south = [(t * tiles + i + 1, (t ^ 2) * tiles + i) for t in range(4) for i in range(tiles - 1)]

    pcs_all = [pcs] + [lax.ppermute(pcs, "tm", [(i, i ^ s) for i in range(4)]) for s in (1, 2, 3)]
    own = spatial_eof.reshape(2, depth, lon)
    mine = [pick_call(own, lat, 0, pcs_all[1])]
    mine.append(pick_call(own, lat, 1, mine[0]))
    crossed = [lax.ppermute(after(m, *pcs_all[2:]), "tm", swap_chip) for m in mine]
    swapped = [lax.ppermute(m, "tm", swap_core) for m in mine]
    oth = lax.ppermute(after(own, pcs_all[1]), "tm", swap_core)

    place = jnp.stack([(tm ^ 2) * day_dev, tm * day_dev, tm]).astype(jnp.int32)
    comp = components_call(after(place, mine[1]), pcs_all, st_eof, share)

    inners = []
    first = 0
    for i, span in enumerate(DAY_GROUPS):
        send, keep = inner_call(comp, own, oth, lat, lon, first, span, LON_BLOCK)
        inners.append((lax.ppermute(send, "tm", swap_chip), keep))
        first += span
        if i == 0:
            comp = after(comp, send, crossed[0])
        if i == 1:
            across = [lax.ppermute(after(c, send), "tm", swap_core) for c in crossed]
            comp = after(comp, send)
            parts = [a for x in range(2) for a in (mine[x], swapped[x], crossed[x], across[x])]
            low, high, ends = edge_call(comp, land_sea, parts, LON_BLOCK)
            halos = [lax.ppermute(low, ("tm", "tile"), north), lax.ppermute(high, ("tm", "tile"), south)]
            comp = after(comp, low, inners[0][0])

    rows = (tile * lat).astype(F32) + jnp.arange(-1, lat + 1, dtype=F32)
    latitude = (-70.0 + 140.0 * (rows + 0.5) / (lat * tiles)) * (math.pi / 180.0)
    cosine = jnp.cos(latitude)
    coef = jnp.stack([cosine[2:], cosine[:-2], 0.5 / cosine[1:-1]])
    coef = jnp.broadcast_to(coef[:, :, None], (3, lat, 128))

    outs = []
    first = 0
    for span, (inner, keep) in zip(DAY_GROUPS, inners):
        outs = curl_call(keep, inner, ends, halos, land_sea, coef, outs, lat, day_dev, first, span)
        first += span
    return tuple(outs)


def solution(mesh):
    return jax.shard_map(
        shards,
        mesh=mesh,
        in_specs=(P(None, "tm"), P(), P(None, "tm", "tile", None), P("tile", None)),
        out_specs=(P("tm", "tile", None), P("tm", "tile", None)),
        check_vma=False,
    )
```
